512 devices in a mesh: box: 128 (over z, y, x_hi), seg: 4 (over x_lo, core).
Axes of the slice: x: 4 (x_hi: 2, x_lo: 2; x = x_hi * 2 + x_lo), y: 8, z: 8, core: 2. Of those that a mesh axis runs over, the one named last changes fastest.
Arguments:
- density_zero: bfloat16 [65536, 64], P('box'), may hold values from 0.25 to 4
- offsets: int32 [256, 4], P('box'), may hold values from -4 to 4, as said below
- start_one: int32 [128, 4, 1024], P('box', 'seg'), may hold values from 0 to 511, as said below
- slot_one: int32 [128, 4, 1024], P('box', 'seg'), may hold values from 0 to 3
- end_one: int32 [128, 4, 1024], P('box', 'seg'), may hold values from 0 to 255
- weight_one: float32 [128, 4, 1024], P('box', 'seg'), may hold values from 0.25 to 4
- start_two: int32 [128, 4, 1024], P('box', 'seg'), may hold values from 0 to 511, as said below
- slot_two: int32 [128, 4, 1024], P('box', 'seg'), may hold values from 0 to 3
- end_two: int32 [128, 4, 1024], P('box', 'seg'), may hold values from 0 to 255
- weight_two: float32 [128, 4, 1024], P('box', 'seg'), may hold values from 0.25 to 4
Outputs:
- density_one: bfloat16 [65536, 64], P('box')
- density_two: bfloat16 [65536, 64], P('box')
The draws below stay inside these ranges and needn't reach their ends.
Inputs may be any that keep to these rules, and one draw needn't show every extreme that they name: `offsets`: in each row, the 4 entries are distinct. `start_one`: for every [g, l], each of the 512 rows appears exactly 1024 // 512 times. `start_two`: for every [g, l], each of the 512 rows appears exactly 1024 // 512 times.
All inputs are finite; a program needn't handle non-finite values.
Results may differ from the reference program's by a relative error of at most 0.009.
Values may be sent and summed in bfloat16 or wider, within the bound.
No kernel may reach another device: no remote copies, remote signals or barrier semaphores. Data moves between devices by JAX's collectives and lax.ppermute only.
A program may use at most 64 MiB of HBM per device.

```python
import math
import jax
import jax.numpy as jnp

BLOCK = 256
COLS = 64
K = 4
REACH = 2
RBD = 2
SEG_DEV = 1024
GROUPS = 128
LANES = 4
BLOCKS = 256
BOXES = 65536


def draw_rows(key):
    keys = jax.random.split(key, GROUPS * LANES)
    base = jnp.tile(jnp.arange(RBD * BLOCK, dtype=jnp.int32), SEG_DEV // (RBD * BLOCK))
    rows = jax.vmap(lambda one: jax.random.permutation(one, base))(keys)
    return rows.reshape(GROUPS, LANES, SEG_DEV).astype(jnp.int32)


def draw_start_one(key, part):
    return draw_rows(jax.random.fold_in(key, 11))


def draw_start_two(key, part):
    return draw_rows(jax.random.fold_in(key, 23))


def draw_offsets(key, part):
    keys = jax.random.split(jax.random.fold_in(key, 37), BLOCKS)
    span = 2 * REACH * RBD + 1
    picks = jax.vmap(lambda one: jax.random.permutation(one, jnp.arange(span, dtype=jnp.int32))[:K])(keys)
    return (picks - REACH * RBD).astype(jnp.int32)


def touch_ends(values, own_key, smallest, largest):
    extent = values.shape
    index_at = [jax.random.randint(jax.random.fold_in(own_key, axis), (), 0, extent[axis]) for axis in range(len(extent))]
    values = values.at[tuple(index_at)].set(smallest)
    longest = extent.index(max(extent))
    index_at[longest] = (index_at[longest] + 1) % extent[longest]
    return values.at[tuple(index_at)].set(largest)


def shard_levels(own_key, shape, cuts, smallest, high):
    def one(dim, parts):
        steps = jax.random.uniform(jax.random.fold_in(jax.random.fold_in(own_key, 6), dim), (parts,), jnp.float32, smallest / len(cuts), high / len(cuts))
        return jnp.repeat(jnp.exp(steps), shape[dim] // parts).reshape((-1,) + (1,) * (len(shape) - dim - 1))

    loudness = one(*cuts[0])
    for cut in cuts[1:]:
        loudness = loudness * one(*cut)
    return loudness


def setup_inputs(seed: int = 0) -> dict:
    seeds = jax.random.split(jax.random.key(seed), 11)
    density_zero = jnp.clip(jnp.exp(math.log(4.0) - 2.7725887 * jax.random.uniform(seeds[0], (BOXES, COLS), jnp.float32) ** shard_levels(seeds[0], (BOXES, COLS), ((0, 128),), -0.2, 0.2)), 0.25, 4.0).astype(jnp.bfloat16)
    offsets = draw_offsets(jax.random.fold_in(seeds[10], 71), 0)
    start_one = draw_start_one(jax.random.fold_in(seeds[10], 71), 0)
    slot_one = touch_ends(jax.random.randint(seeds[3], (GROUPS, LANES, SEG_DEV), 0, K), jax.random.fold_in(seeds[3], 1), 0, K - 1).astype(jnp.int32)
    end_one = touch_ends(jax.random.randint(seeds[4], (GROUPS, LANES, SEG_DEV), 0, BLOCK), jax.random.fold_in(seeds[4], 1), 0, BLOCK - 1).astype(jnp.int32)
    weight_one = jnp.clip(jnp.exp(math.log(4.0) - 2.7725887 * jax.random.uniform(seeds[5], (GROUPS, LANES, SEG_DEV), jnp.float32) ** shard_levels(seeds[5], (GROUPS, LANES, SEG_DEV), ((0, 128), (1, 4)), -0.2, 0.2)), 0.25, 4.0)
    start_two = draw_start_two(jax.random.fold_in(seeds[10], 71), 0)
    slot_two = touch_ends(jax.random.randint(seeds[7], (GROUPS, LANES, SEG_DEV), 0, K), jax.random.fold_in(seeds[7], 1), 0, K - 1).astype(jnp.int32)
    end_two = touch_ends(jax.random.randint(seeds[8], (GROUPS, LANES, SEG_DEV), 0, BLOCK), jax.random.fold_in(seeds[8], 1), 0, BLOCK - 1).astype(jnp.int32)
    weight_two = jnp.clip(jnp.exp(math.log(4.0) - 2.7725887 * jax.random.uniform(seeds[9], (GROUPS, LANES, SEG_DEV), jnp.float32) ** shard_levels(seeds[9], (GROUPS, LANES, SEG_DEV), ((0, 128), (1, 4)), -0.2, 0.2)), 0.25, 4.0)
    return {"density_zero": density_zero, "offsets": offsets, "start_one": start_one, "slot_one": slot_one, "end_one": end_one, "weight_one": weight_one, "start_two": start_two, "slot_two": slot_two, "end_two": end_two, "weight_two": weight_two}


def one_day(density, offsets, start, slot, end, weight):
    group_rows = RBD * BLOCK
    base = (jnp.arange(GROUPS, dtype=jnp.int32) * group_rows)[:, None, None]
    boxes = (start + base).reshape(-1).astype(jnp.int32)
    row_block = boxes // BLOCK
    chosen = offsets[row_block, slot.reshape(-1)]
    col_block = (row_block + chosen) % BLOCKS
    ends = (col_block * BLOCK + end.reshape(-1)).astype(jnp.int32)
    weights = weight.reshape(-1)
    totals = jax.ops.segment_sum(weights, boxes, num_segments=BOXES)
    scaled = (density.astype(jnp.float32) / totals[:, None]).astype(jnp.bfloat16)
    carried = scaled.astype(jnp.float32)[boxes] * weights[:, None]
    return jax.ops.segment_sum(carried, ends, num_segments=BOXES).astype(jnp.bfloat16)


def reference(density_zero, offsets, start_one, slot_one, end_one, weight_one, start_two, slot_two, end_two, weight_two):
    density_one = one_day(density_zero, offsets, start_one, slot_one, end_one, weight_one)
    density_two = one_day(density_one, offsets, start_two, slot_two, end_two, weight_two)
    return (density_one, density_two)
```

```python
import functools

import jax
import jax.numpy as jnp
from jax import lax
from jax.experimental import pallas as pl
from jax.experimental.pallas import tpu as pltpu
from jax.sharding import PartitionSpec as P

F32 = jnp.float32
BF16 = jnp.bfloat16
BLOCK = 256
COLS = 64
WIDTH = 4
AXES = ("box", "seg")


def place():
    box = lax.axis_index("box")
    core = lax.axis_index("seg") % 2
    pair = box // 2
    return pair, box % 2, core, 1 - (pair + core) % 2


def pair_groups(boxes):
    pairs = boxes // 2
    groups = []
    for first in range(pairs):
        second = (first + 1) % pairs
        for chip in range(4):
            core = first % 2
            groups.append([first * 8 + chip * 2 + core, second * 8 + chip * 2 + core])
    return groups


def core_groups(boxes):
    return [[2 * chip, 2 * chip + 1] for chip in range(boxes * 2)]


def half_groups(boxes):
    groups = []
    for pair in range(boxes // 2):
        for core in range(2):
            groups.append([pair * 8 + 2 + core, pair * 8 + 4 + core])
            groups.append([pair * 8 + core, pair * 8 + 6 + core])
    return groups


def iota(shape, dim):
    return lax.broadcasted_iota(jnp.int32, shape, dim)


def sort_kernel(*refs):
    *ins, out_ref, pick_ref = refs
    rows = out_ref.shape[1]
    count = ins[0].shape[-1]
    step = 64
    lane = iota((step, count), 1).astype(F32)
    for day in range(2):
        start, slot, end, weight = (ref[0] for ref in ins[4 * day : 4 * day + 4])
        for at in range(0, rows, step):
            hit = start == iota((step, count), 0) + at
            first = jnp.min(jnp.where(hit, lane, float(count)), axis=1, keepdims=True)
            last = jnp.max(jnp.where(hit, lane, -1.0), axis=1, keepdims=True)
            pick_ref[at : at + step, :] = jnp.where(lane == first, 1.0, 0.0).astype(BF16)
            pick_ref[rows + at : rows + at + step, :] = jnp.where(lane == last, 1.0, 0.0).astype(BF16)
        high = weight.astype(BF16).astype(F32)
        middle = (weight - high).astype(BF16).astype(F32)
        low = weight - high - middle
        zero = jnp.zeros_like(weight)
        load = jnp.concatenate(
            [end.astype(F32), slot.astype(F32), high, middle, low, zero, zero, zero], axis=0
        ).astype(BF16)
        got = lax.dot_general(
            load, pick_ref[...], (((1,), (1,)), ((), ())), preferred_element_type=F32
        )
        target = got[1:2] * float(BLOCK) + got[0:1]
        total = got[2:3] + got[3:4] + got[4:5]
        out_ref[4 * day : 4 * day + 4, :] = jnp.concatenate(
            [target[:, :rows], target[:, rows:], total[:, :rows], total[:, rows:]], axis=0
        )


def counts_block(keys, weights, counts_ref):
    step = 32
    width = counts_ref.shape[1]
    for at in range(0, BLOCK, step):
        ends = (iota((step, width), 0) + at).astype(F32)
        total = None
        for key, weight in zip(keys, weights):
            term = jnp.where(key == ends, weight, 0.0)
            total = term if total is None else total + term
        counts_ref[at : at + step, :] = total.astype(BF16)


def first_kernel(lists_ref, density_ref, offsets_ref, side_ref, own_ref, meta_ref, key_ref, weight_ref, spread_ref, counts_ref, sums_ref):
    pair, half, core, ahead = place()
    lanes = lists_ref.shape[0]
    rows = lists_ref.shape[2]
    for day in range(2):
        keys = jnp.concatenate([lists_ref[lane, 4 * day : 4 * day + 2, :] for lane in range(lanes)], axis=0)
        weights = jnp.concatenate([lists_ref[lane, 4 * day + 2 : 4 * day + 4, :] for lane in range(lanes)], axis=0)
        weights = weights / jnp.sum(weights, axis=0, keepdims=True)
        if day == 0:
            key_ref[...] = keys
            weight_ref[...] = weights
        else:
            slots = jnp.floor(keys * (1.0 / BLOCK))
            ends = keys - slots * float(BLOCK)
            offs = jnp.concatenate(
                [jnp.full((1, 128), offsets_ref[j, s].astype(F32), F32) for j in range(2) for s in range(WIDTH)], axis=0
            )
            for part in range(rows // 128):
                cut = slice(128 * part, 128 * part + 128)
                meta_ref[32 * part : 32 * part + 32, :] = jnp.concatenate(
                    [ends[:, cut], slots[:, cut], weights[:, cut], offs], axis=0
                ).astype(BF16)
    zero = jnp.zeros((BLOCK, COLS), BF16)
    for j in range(2):
        block = density_ref[BLOCK * j : BLOCK * j + BLOCK, :]
        spread_ref[j, 0] = jnp.concatenate([block, zero], axis=1)
        spread_ref[j, 1] = jnp.concatenate([zero, block], axis=1)
    sums_ref[...] = jnp.zeros_like(sums_ref)
    for j in range(2):

        @pl.loop(0, WIDTH)
        def _(s):
            block = 2 * half + j + offsets_ref[j, s]
            where = jnp.where(block < 0, 0, jnp.where(block >= 4, 1, 2))
            inside = where == 2
            mine = jnp.logical_or(where == ahead, jnp.logical_and(inside, core == j))

            @pl.when(mine)
            def _():
                cut = slice(BLOCK * j, BLOCK * j + BLOCK)
                base = (s * BLOCK).astype(F32)
                keys = [key_ref[k : k + 1, cut] - base for k in range(2 * lanes)]
                weights = [weight_ref[k : k + 1, cut] for k in range(2 * lanes)]
                counts_block(keys, weights, counts_ref)
                spot = block & 3
                pushed = jnp.dot(counts_ref[...], spread_ref[j, spot >> 1], preferred_element_type=F32)
                at = jnp.where(inside, 1, 0)
                sums_ref[at, spot & 1] += pushed

    for part in range(2):
        cut = slice(BLOCK * part, BLOCK * part + BLOCK)
        side_ref[cut, :] = sums_ref[0, part].astype(BF16)
        own_ref[cut, :] = sums_ref[1, part]


def second_kernel(parts_ref, density_ref, side_ref, own_ref, spread_ref, counts_ref, sums_ref):
    pair, half, core, ahead = place()
    rows = 2 * BLOCK
    total = parts_ref[0, :rows, :].astype(F32) + parts_ref[1, :rows, :].astype(F32)
    total = total.astype(BF16).astype(F32)
    density_ref[...] = jnp.where(half == 0, total[:, :COLS], total[:, COLS:]).astype(BF16)
    left = iota((BLOCK, 128), 1) < COLS
    for j in range(4):
        block = total[BLOCK * (j & 1) : BLOCK * (j & 1) + BLOCK, :]
        kept = jnp.where(left if j < 2 else jnp.logical_not(left), block, 0.0)
        turned = pltpu.roll(kept, COLS, 1)
        spread_ref[j, j >> 1] = kept.astype(BF16)
        spread_ref[j, 1 - (j >> 1)] = turned.astype(BF16)
    sums_ref[...] = jnp.zeros_like(sums_ref)
    for j in range(4):
        group = j >> 1
        at = rows + 64 * (j & 1)
        lists = [parts_ref[group, at + 32 * q : at + 32 * q + 32, :].astype(F32) for q in range(2)]
        for s in range(WIDTH):
            offset = lists[0][24 + 4 * (j & 1) + s, 0].astype(jnp.int32)
            block = j + offset
            where = jnp.where(block < 0, 0, jnp.where(block >= 4, 1, 2))
            inside = where == 2
            mine = jnp.logical_or(where == ahead, jnp.logical_and(inside, core == (j & 1)))
            mine = jnp.logical_and(mine, ((block >> 1) & 1) == half)

            @pl.when(mine)
            def _():
                keys, weights = [], []
                for k in range(8):
                    pieces = [
                        (one[k : k + 1, :] - jnp.where(one[8 + k : 9 + k, :] == float(s), 0.0, 512.0), one[16 + k : 17 + k, :])
                        for one in lists
                    ]
                    keys.append(jnp.concatenate([piece[0] for piece in pieces], axis=1))
                    weights.append(jnp.concatenate([piece[1] for piece in pieces], axis=1))
                counts_block(keys, weights, counts_ref)
                pushed = jnp.dot(counts_ref[...], spread_ref[j, block & 1], preferred_element_type=F32)
                sums_ref[jnp.where(inside, 1, 0)] += pushed

    side_ref[...] = sums_ref[0].astype(BF16)
    own_ref[...] = sums_ref[1]


VMEM = pl.BlockSpec(memory_space=pltpu.VMEM)
SMEM = pl.BlockSpec(memory_space=pltpu.SMEM)


def call(kernel, name, ins, outs, scratch):
    return pl.pallas_call(
        kernel,
        out_shape=outs,
        in_specs=ins,
        out_specs=jax.tree.map(lambda _: VMEM, outs),
        scratch_shapes=scratch,
        compiler_params=pltpu.CompilerParams(vmem_limit_bytes=32 * 1024 * 1024),
        name=name,
    )


def body(density, offsets, *segments):
    boxes = lax.axis_size("box")
    rows = density.shape[0]
    count = segments[0].shape[-1]
    gather = functools.partial(lax.all_gather, axis_name=AXES)
    pair, half, core, ahead = place()

    lists = call(
        sort_kernel,
        "sort",
        [VMEM] * 8,
        jax.ShapeDtypeStruct((8, rows), F32),
        [pltpu.VMEM((2 * rows, count), BF16)],
    )(*[member.reshape(1, 1, count) for member in segments])
    lists = lax.all_gather(lists, "seg")
    side, own, meta = call(
        first_kernel,
        "first",
        [VMEM, VMEM, SMEM],
        (
            jax.ShapeDtypeStruct((rows, 128), BF16),
            jax.ShapeDtypeStruct((rows, 128), F32),
            jax.ShapeDtypeStruct((128, 128), BF16),
        ),
        [
            pltpu.VMEM((8, rows), F32),
            pltpu.VMEM((8, rows), F32),
            pltpu.VMEM((2, 2, BLOCK, 128), BF16),
            pltpu.VMEM((BLOCK, BLOCK), BF16),
            pltpu.VMEM((2, 2, BLOCK, 128), F32),
        ],
    )(lists, density, offsets)
    sides = gather(side, axis_index_groups=pair_groups(boxes))
    came = jnp.where(ahead == 1, sides[1], sides[0])
    mixed = (own + came.astype(F32)).astype(BF16)
    both = gather(mixed, axis_index_groups=core_groups(boxes))
    summed = (both[0].astype(F32) + both[1].astype(F32)).astype(BF16)
    parts = gather(jnp.concatenate([summed, meta], axis=0), axis_index_groups=half_groups(boxes))
    density_one, side, own = call(
        second_kernel,
        "second",
        [VMEM],
        (
            jax.ShapeDtypeStruct((rows, COLS), BF16),
            jax.ShapeDtypeStruct((BLOCK, 128), BF16),
            jax.ShapeDtypeStruct((BLOCK, 128), F32),
        ),
        [
            pltpu.VMEM((4, 2, BLOCK, 128), BF16),
            pltpu.VMEM((BLOCK, BLOCK), BF16),
            pltpu.VMEM((2, BLOCK, 128), F32),
        ],
    )(parts)
    sides = gather(side, axis_index_groups=pair_groups(boxes))
    came = jnp.where(ahead == 1, sides[1], sides[0])
    both = gather(own + came.astype(F32), axis_index_groups=core_groups(boxes))
    summed = (both[0] + both[1]).astype(BF16)
    density_two = jnp.concatenate([summed[:, :COLS], summed[:, COLS:]], axis=0)
    return density_one, density_two


def solution(mesh):
    boxed = P("box", None)
    lined = P("box", "seg", None)
    return jax.shard_map(
        body,
        mesh=mesh,
        in_specs=(boxed, boxed) + (lined,) * 8,
        out_specs=(boxed, boxed),
        check_vma=False,
    )
```

```python
import functools

import jax
import jax.numpy as jnp
from jax import lax
from jax.experimental import pallas as pl
from jax.experimental.pallas import tpu as pltpu
from jax.sharding import PartitionSpec as P

F32 = jnp.float32
BF16 = jnp.bfloat16
BLOCK = 256
COLS = 64
WIDTH = 4
AXES = ("box", "seg")


def place():
    box = lax.axis_index("box")
    core = lax.axis_index("seg") % 2
    pair = box // 2
    return pair, box % 2, core, 1 - (pair + core) % 2


def pair_groups(boxes):
    pairs = boxes // 2
    groups = []
    for first in range(pairs):
        second = (first + 1) % pairs
        for chip in range(4):
            core = first % 2
            groups.append([first * 8 + chip * 2 + core, second * 8 + chip * 2 + core])
    return groups


def core_groups(boxes):
    return [[2 * chip, 2 * chip + 1] for chip in range(boxes * 2)]


def half_groups(boxes):
    groups = []
    for pair in range(boxes // 2):
        for core in range(2):
            groups.append([pair * 8 + 2 + core, pair * 8 + 4 + core])
            groups.append([pair * 8 + core, pair * 8 + 6 + core])
    return groups


def iota(shape, dim):
    return lax.broadcasted_iota(jnp.int32, shape, dim)


def across(left, right):
    return lax.dot_general(left, right, (((1,), (1,)), ((), ())), preferred_element_type=F32)


def sort_kernel(*refs):
    *ins, offsets_ref, out_ref, marks_ref, pick_ref = refs
    rows = out_ref.shape[1]
    count = ins[0].shape[-1]
    step = 64
    lane = iota((step, count), 1).astype(F32)
    offs = offsets_ref[...].astype(F32)
    marks_ref[...] = jnp.concatenate(
        [jnp.broadcast_to(offs[j : j + 1, s : s + 1], (1, 128)) for j in range(2) for s in range(WIDTH)], axis=0
    )
    for day in range(2):
        start, slot, end, weight = (ref[0] for ref in ins[4 * day : 4 * day + 4])
        for at in range(0, rows, step):
            hit = start == iota((step, count), 0) + at
            first = jnp.min(jnp.where(hit, lane, float(count)), axis=1, keepdims=True)
            last = jnp.max(jnp.where(hit, lane, -1.0), axis=1, keepdims=True)
            pick_ref[at : at + step, :] = jnp.where(lane == first, 1.0, 0.0).astype(BF16)
            pick_ref[rows + at : rows + at + step, :] = jnp.where(lane == last, 1.0, 0.0).astype(BF16)
        high = weight.astype(BF16).astype(F32)
        middle = (weight - high).astype(BF16).astype(F32)
        low = weight - high - middle
        zero = jnp.zeros_like(weight)
        load = jnp.concatenate(
            [end.astype(F32), slot.astype(F32), high, middle, low, zero, zero, zero], axis=0
        ).astype(BF16)
        got = across(load, pick_ref[...])
        target = got[1:2] * float(BLOCK) + got[0:1]
        total = got[2:3] + got[3:4] + got[4:5]
        out_ref[4 * day : 4 * day + 4, :] = jnp.concatenate(
            [target[:, :rows], target[:, rows:], total[:, :rows], total[:, rows:]], axis=0
        )


def split_work(blocks, half_only, ahead):
    places = []
    for block in blocks:
        place_of = jnp.where(block < 0, 0, jnp.where(block >= 4, 1, 2))
        if half_only is not None:
            place_of = jnp.where(((block >> 1) & 1) == half_only, place_of, 3)
        places.append(place_of)
    behind, front, inside = (sum((p == kind).astype(jnp.int32) for p in places) for kind in range(3))
    share = jnp.clip(((behind + front + inside + 1) >> 1) - front, 0, inside)
    mine, seen = [], 0
    for p in places:
        is_inside = p == 2
        taker = jnp.where(seen < share, 1, 0)
        mine.append(jnp.logical_or(p == ahead, jnp.logical_and(is_inside, taker == ahead)))
        seen = seen + is_inside.astype(jnp.int32)
    return places, mine


def push_block(key_ref, weight_ref, part, s, density, counts_ref, sum_ref):
    cut = slice(BLOCK * part, BLOCK * part + BLOCK)
    step = 16
    keys, weights = [], []
    for k in range(key_ref.shape[0]):
        key = key_ref[k : k + 1, cut] - float(s * BLOCK)
        keys.append(jnp.broadcast_to(key, (step, BLOCK)).astype(BF16))
        weights.append(jnp.broadcast_to(weight_ref[k : k + 1, cut], (step, BLOCK)).astype(BF16))
    first = iota((step, BLOCK), 0).astype(F32)
    zero = jnp.zeros((step, BLOCK), BF16)
    for at in range(0, BLOCK, step):
        ends = (first + float(at)).astype(BF16)
        total = None
        for key, weight in zip(keys, weights):
            term = jnp.where(key == ends, weight, zero)
            total = term if total is None else total + term
        counts_ref[at : at + step, :] = total
    sum_ref[...] += across(density, counts_ref[...])


def first_kernel(lists_ref, density_ref, marks_ref, side_ref, own_ref, meta_ref, key_ref, weight_ref, counts_ref, sums_ref):
    pair, half, core, ahead = place()
    lanes = lists_ref.shape[0]
    rows = lists_ref.shape[2]
    marks = marks_ref[...]
    whole = marks.astype(jnp.int32)
    blocks = [2 * half + i // WIDTH + whole[i, 0] for i in range(2 * WIDTH)]
    places, mine = split_work(blocks, None, ahead)
    for day in range(2):
        keys = jnp.concatenate([lists_ref[lane, 4 * day : 4 * day + 2, :] for lane in range(lanes)], axis=0)
        weights = jnp.concatenate([lists_ref[lane, 4 * day + 2 : 4 * day + 4, :] for lane in range(lanes)], axis=0)
        weights = weights / jnp.sum(weights, axis=0, keepdims=True)
        if day == 0:
            key_ref[...] = keys
            weight_ref[...] = weights
        else:
            slots = jnp.floor(keys * (1.0 / BLOCK))
            ends = keys - slots * float(BLOCK)
            wide = jnp.concatenate([marks, marks], axis=1)
            for part in range(2):
                cut = slice(BLOCK * part, BLOCK * part + BLOCK)
                meta_ref[32 * part : 32 * part + 32, :] = jnp.concatenate(
                    [ends[:, cut], slots[:, cut], weights[:, cut], wide], axis=0
                ).astype(BF16)
    sums_ref[...] = jnp.zeros_like(sums_ref)
    for j in range(2):
        for s in range(WIDTH):
            number = WIDTH * j + s

            @pl.when(mine[number])
            def _():
                at = jnp.where(places[number] == 2, 1, 0)
                density = density_ref[:, BLOCK * j : BLOCK * j + BLOCK]
                push_block(key_ref, weight_ref, j, s, density, counts_ref, sums_ref.at[at, blocks[number] & 3])

    for spot in range(4):
        cut = slice(COLS * spot, COLS * spot + COLS)
        side_ref[cut, :] = sums_ref[0, spot].astype(BF16)
        own_ref[cut, :] = sums_ref[1, spot]


def second_kernel(parts_ref, density_ref, side_ref, own_ref, stage_ref, key_ref, weight_ref, from_ref, counts_ref, sums_ref, sem):
    pair, half, core, ahead = place()
    wide = 4 * COLS
    total = parts_ref[0, :wide, :].astype(F32) + parts_ref[1, :wide, :].astype(F32)
    for j in range(4):
        from_ref[j] = total[COLS * j : COLS * j + COLS].astype(BF16)
    for part in range(2):
        stage_ref[:, BLOCK * part : BLOCK * part + BLOCK] = from_ref[2 * half + part]
    store = pltpu.make_async_copy(stage_ref, density_ref, sem)
    store.start()
    blocks = []
    for group in range(2):
        for part in range(2):
            piece = parts_ref[group, wide + 32 * part : wide + 32 * part + 32, :].astype(F32)
            cut = slice(BLOCK * part, BLOCK * part + BLOCK)
            key_ref[group, :, cut] = piece[8:16] * float(BLOCK) + piece[0:8]
            weight_ref[group, :, cut] = piece[16:24]
            if part == 0:
                whole = piece[24:32, :128].astype(jnp.int32)
                blocks += [2 * group + i // WIDTH + whole[i, 0] for i in range(2 * WIDTH)]
    places, mine = split_work(blocks, half, ahead)
    sums_ref[...] = jnp.zeros_like(sums_ref)
    for j in range(4):
        for s in range(WIDTH):
            number = WIDTH * j + s

            @pl.when(mine[number])
            def _():
                at = jnp.where(places[number] == 2, 1, 0)
                push_block(
                    key_ref.at[j >> 1], weight_ref.at[j >> 1], j & 1, s, from_ref[j], counts_ref, sums_ref.at[at, blocks[number] & 1]
                )

    for spot in range(2):
        cut = slice(COLS * spot, COLS * spot + COLS)
        side_ref[cut, :] = sums_ref[0, spot].astype(BF16)
        own_ref[cut, :] = sums_ref[1, spot]
    store.wait()


def last_kernel(both_ref, density_ref, stage_ref, sem):
    total = (both_ref[0] + both_ref[1]).astype(BF16)
    stage_ref[:, :BLOCK] = total[:COLS]
    stage_ref[:, BLOCK:] = total[COLS:]
    store = pltpu.make_async_copy(stage_ref, density_ref, sem)
    store.start()
    store.wait()


VMEM = pl.BlockSpec(memory_space=pltpu.VMEM)
ANY = pl.BlockSpec(memory_space=pl.ANY)


def call(kernel, name, outs, out_specs, scratch):
    return pl.pallas_call(
        kernel,
        out_shape=outs,
        out_specs=out_specs,
        scratch_shapes=scratch,
        compiler_params=pltpu.CompilerParams(vmem_limit_bytes=32 * 1024 * 1024),
        name=name,
    )


def shaped(*shape, dtype=F32):
    return jax.ShapeDtypeStruct(shape, dtype)


def body(density, offsets, *segments):
    boxes = lax.axis_size("box")
    rows = density.shape[0]
    count = segments[0].shape[-1]
    gather = functools.partial(lax.all_gather, axis_name=AXES)
    pair, half, core, ahead = place()

    lists, marks = call(
        sort_kernel,
        "sort",
        (shaped(8, rows), shaped(8, 128)),
        (VMEM, VMEM),
        [pltpu.VMEM((2 * rows, count), BF16)],
    )(*[member.reshape(1, 1, count) for member in segments], offsets)
    lists = lax.all_gather(lists, "seg")
    side, own, meta = call(
        first_kernel,
        "first",
        (shaped(4 * COLS, BLOCK, dtype=BF16), shaped(4 * COLS, BLOCK), shaped(64, BLOCK, dtype=BF16)),
        (VMEM, VMEM, VMEM),
        [
            pltpu.VMEM((8, rows), F32),
            pltpu.VMEM((8, rows), F32),
            pltpu.VMEM((BLOCK, BLOCK), BF16),
            pltpu.VMEM((2, 4, COLS, BLOCK), F32),
        ],
    )(lists, density.T, marks)
    sides = gather(side, axis_index_groups=pair_groups(boxes))
    came = jnp.where(ahead == 1, sides[1], sides[0])
    mixed = (own + came.astype(F32)).astype(BF16)
    both = gather(mixed, axis_index_groups=core_groups(boxes))
    summed = (both[0].astype(F32) + both[1].astype(F32)).astype(BF16)
    parts = gather(jnp.concatenate([summed, meta], axis=0), axis_index_groups=half_groups(boxes))
    density_one, side, own = call(
        second_kernel,
        "second",
        (shaped(COLS, rows, dtype=BF16), shaped(2 * COLS, BLOCK, dtype=BF16), shaped(2 * COLS, BLOCK)),
        (ANY, VMEM, VMEM),
        [
            pltpu.VMEM((COLS, rows), BF16),
            pltpu.VMEM((2, 8, rows), F32),
            pltpu.VMEM((2, 8, rows), F32),
            pltpu.VMEM((4, COLS, BLOCK), BF16),
            pltpu.VMEM((BLOCK, BLOCK), BF16),
            pltpu.VMEM((2, 2, COLS, BLOCK), F32),
            pltpu.SemaphoreType.DMA,
        ],
    )(parts)
    sides = gather(side, axis_index_groups=pair_groups(boxes))
    came = jnp.where(ahead == 1, sides[1], sides[0])
    both = gather(own + came.astype(F32), axis_index_groups=core_groups(boxes))
    density_two = call(
        last_kernel,
        "last",
        shaped(COLS, rows, dtype=BF16),
        ANY,
        [pltpu.VMEM((COLS, rows), BF16), pltpu.SemaphoreType.DMA],
    )(both)
    return density_one.T, density_two.T


def solution(mesh):
    boxed = P("box", None)
    lined = P("box", "seg", None)
    return jax.shard_map(
        body,
        mesh=mesh,
        in_specs=(boxed, boxed) + (lined,) * 8,
        out_specs=(boxed, boxed),
        check_vma=False,
    )
```

```python
import functools

import jax
import jax.numpy as jnp
from jax import lax
from jax.experimental import pallas as pl
from jax.experimental.pallas import tpu as pltpu
from jax.sharding import PartitionSpec as P

F32 = jnp.float32
BF16 = jnp.bfloat16
BLOCK = 256
COLS = 64
WIDTH = 4
AXES = ("box", "seg")


def place():
    box = lax.axis_index("box")
    core = lax.axis_index("seg") % 2
    pair = box // 2
    return pair, box % 2, core, 1 - (pair + core) % 2


def pair_groups(boxes):
    pairs = boxes // 2
    groups = []
    for first in range(pairs):
        second = (first + 1) % pairs
        for chip in range(4):
            core = first % 2
            groups.append([first * 8 + chip * 2 + core, second * 8 + chip * 2 + core])
    return groups


def core_groups(boxes):
    return [[2 * chip, 2 * chip + 1] for chip in range(boxes * 2)]


def half_groups(boxes):
    groups = []
    for pair in range(boxes // 2):
        groups.append([pair * 8 + i for i in (2, 3, 4, 5)])
        groups.append([pair * 8 + i for i in (0, 1, 6, 7)])
    return groups


def iota(shape, dim):
    return lax.broadcasted_iota(jnp.int32, shape, dim)


def across(left, right):
    return lax.dot_general(left, right, (((1,), (1,)), ((), ())), preferred_element_type=F32)


def sort_kernel(*refs):
    *ins, offsets_ref, out_ref, marks_ref, pick_ref = refs
    rows = out_ref.shape[1]
    count = ins[0].shape[-1]
    step = 64
    lane = iota((step, count), 1).astype(F32)
    offs = offsets_ref[...].astype(F32)
    marks_ref[...] = jnp.concatenate(
        [jnp.broadcast_to(offs[j : j + 1, s : s + 1], (1, 128)) for j in range(2) for s in range(WIDTH)], axis=0
    )
    for day in range(2):
        start, slot, end, weight = (ref[0] for ref in ins[4 * day : 4 * day + 4])
        for at in range(0, rows, step):
            hit = start == iota((step, count), 0) + at
            first = jnp.min(jnp.where(hit, lane, float(count)), axis=1, keepdims=True)
            last = jnp.max(jnp.where(hit, lane, -1.0), axis=1, keepdims=True)
            pick_ref[at : at + step, :] = jnp.where(lane == first, 1.0, 0.0).astype(BF16)
            pick_ref[rows + at : rows + at + step, :] = jnp.where(lane == last, 1.0, 0.0).astype(BF16)
        high = weight.astype(BF16).astype(F32)
        middle = (weight - high).astype(BF16).astype(F32)
        low = weight - high - middle
        zero = jnp.zeros_like(weight)
        load = jnp.concatenate(
            [end.astype(F32), slot.astype(F32), high, middle, low, zero, zero, zero], axis=0
        ).astype(BF16)
        got = across(load, pick_ref[...])
        target = got[1:2] * float(BLOCK) + got[0:1]
        total = got[2:3] + got[3:4] + got[4:5]
        out_ref[4 * day : 4 * day + 4, :] = jnp.concatenate(
            [target[:, :rows], target[:, rows:], total[:, :rows], total[:, rows:]], axis=0
        )


def split_work(blocks, half_only, ahead):
    places = []
    for block in blocks:
        place_of = jnp.where(block < 0, 0, jnp.where(block >= 4, 1, 2))
        if half_only is not None:
            place_of = jnp.where(((block >> 1) & 1) == half_only, place_of, 3)
        places.append(place_of)
    behind, front, inside = (sum((p == kind).astype(jnp.int32) for p in places) for kind in range(3))
    share = jnp.clip(((behind + front + inside + 1) >> 1) - front, 0, inside)
    mine, seen = [], 0
    for p in places:
        is_inside = p == 2
        taker = jnp.where(seen < share, 1, 0)
        mine.append(jnp.logical_or(p == ahead, jnp.logical_and(is_inside, taker == ahead)))
        seen = seen + is_inside.astype(jnp.int32)
    return places, mine


def push_block(key_ref, weight_ref, part, s, density, counts_ref, sum_ref):
    cut = slice(BLOCK * part, BLOCK * part + BLOCK)
    step = 16
    keys, weights = [], []
    for k in range(key_ref.shape[0]):
        key = key_ref[k : k + 1, cut] - float(s * BLOCK)
        keys.append(jnp.broadcast_to(key, (step, BLOCK)).astype(BF16))
        weights.append(jnp.broadcast_to(weight_ref[k : k + 1, cut], (step, BLOCK)).astype(BF16))
    first = iota((step, BLOCK), 0).astype(F32)
    zero = jnp.zeros((step, BLOCK), BF16)
    for at in range(0, BLOCK, step):
        ends = (first + float(at)).astype(BF16)
        total = None
        for key, weight in zip(keys, weights):
            term = jnp.where(key == ends, weight, zero)
            total = term if total is None else total + term
        counts_ref[at : at + step, :] = total
    sum_ref[...] += across(density, counts_ref[...])


def first_kernel(lists_ref, density_ref, marks_ref, side_ref, own_ref, meta_ref, key_ref, weight_ref, counts_ref, sums_ref):
    pair, half, core, ahead = place()
    lanes = lists_ref.shape[0]
    rows = lists_ref.shape[2]
    marks = marks_ref[...]
    whole = marks.astype(jnp.int32)
    blocks = [2 * half + i // WIDTH + whole[i, 0] for i in range(2 * WIDTH)]
    places, mine = split_work(blocks, None, ahead)
    for day in range(2):
        keys = jnp.concatenate([lists_ref[lane, 4 * day : 4 * day + 2, :] for lane in range(lanes)], axis=0)
        weights = jnp.concatenate([lists_ref[lane, 4 * day + 2 : 4 * day + 4, :] for lane in range(lanes)], axis=0)
        weights = weights / jnp.sum(weights, axis=0, keepdims=True)
        if day == 0:
            key_ref[...] = keys
            weight_ref[...] = weights
        else:
            slots = jnp.floor(keys * (1.0 / BLOCK))
            ends = keys - slots * float(BLOCK)
            wide = jnp.concatenate([marks, marks], axis=1)
            picked = [jnp.where(core == 0, one[:, :BLOCK], one[:, BLOCK:]) for one in (ends, slots, weights)]
            meta_ref[...] = jnp.concatenate(picked + [wide], axis=0).astype(BF16)
    sums_ref[...] = jnp.zeros_like(sums_ref)
    for j in range(2):
        for s in range(WIDTH):
            number = WIDTH * j + s

            @pl.when(mine[number])
            def _():
                at = jnp.where(places[number] == 2, 1, 0)
                density = density_ref[:, BLOCK * j : BLOCK * j + BLOCK]
                push_block(key_ref, weight_ref, j, s, density, counts_ref, sums_ref.at[at, blocks[number] & 3])

    for spot in range(4):
        cut = slice(COLS * spot, COLS * spot + COLS)
        side_ref[cut, :] = sums_ref[0, spot].astype(BF16)
        own_ref[cut, :] = sums_ref[1, spot]


def second_kernel(parts_ref, density_ref, side_ref, own_ref, stage_ref, key_ref, weight_ref, from_ref, counts_ref, sums_ref, sem):
    pair, half, core, ahead = place()
    wide = 4 * COLS
    for j in range(4):
        cut = slice(COLS * j, COLS * j + COLS)
        one, two, three, four = (parts_ref[i, cut, :].astype(F32) for i in range(4))
        from_ref[j] = ((one + two) + (three + four)).astype(BF16)
    for part in range(2):
        stage_ref[:, BLOCK * part : BLOCK * part + BLOCK] = from_ref[2 * half + part]
    store = pltpu.make_async_copy(stage_ref, density_ref, sem)
    store.start()
    blocks = []
    for j in range(4):
        piece = parts_ref[j, wide : wide + 32, :].astype(F32)
        cut = slice(BLOCK * (j & 1), BLOCK * (j & 1) + BLOCK)
        key_ref[j >> 1, :, cut] = piece[8:16] * float(BLOCK) + piece[0:8]
        weight_ref[j >> 1, :, cut] = piece[16:24]
        whole = piece[24:32, :128].astype(jnp.int32)
        blocks += [j + whole[WIDTH * (j & 1) + s, 0] for s in range(WIDTH)]
    places, mine = split_work(blocks, half, ahead)
    sums_ref[...] = jnp.zeros_like(sums_ref)
    for j in range(4):
        for s in range(WIDTH):
            number = WIDTH * j + s

            @pl.when(mine[number])
            def _():
                at = jnp.where(places[number] == 2, 1, 0)
                push_block(
                    key_ref.at[j >> 1], weight_ref.at[j >> 1], j & 1, s, from_ref[j], counts_ref, sums_ref.at[at, blocks[number] & 1]
                )

    for spot in range(2):
        cut = slice(COLS * spot, COLS * spot + COLS)
        side_ref[cut, :] = sums_ref[0, spot].astype(BF16)
        own_ref[cut, :] = sums_ref[1, spot]
    store.wait()


def last_kernel(both_ref, density_ref, stage_ref, sem):
    total = (both_ref[0] + both_ref[1]).astype(BF16)
    stage_ref[:, :BLOCK] = total[:COLS]
    stage_ref[:, BLOCK:] = total[COLS:]
    store = pltpu.make_async_copy(stage_ref, density_ref, sem)
    store.start()
    store.wait()


VMEM = pl.BlockSpec(memory_space=pltpu.VMEM)
ANY = pl.BlockSpec(memory_space=pl.ANY)


def call(kernel, name, outs, out_specs, scratch):
    return pl.pallas_call(
        kernel,
        out_shape=outs,
        out_specs=out_specs,
        scratch_shapes=scratch,
        compiler_params=pltpu.CompilerParams(vmem_limit_bytes=32 * 1024 * 1024),
        name=name,
    )


def shaped(*shape, dtype=F32):
    return jax.ShapeDtypeStruct(shape, dtype)


def body(density, offsets, *segments):
    boxes = lax.axis_size("box")
    rows = density.shape[0]
    count = segments[0].shape[-1]
    gather = functools.partial(lax.all_gather, axis_name=AXES)
    pair, half, core, ahead = place()

    lists, marks = call(
        sort_kernel,
        "sort",
        (shaped(8, rows), shaped(8, 128)),
        (VMEM, VMEM),
        [pltpu.VMEM((2 * rows, count), BF16)],
    )(*[member.reshape(1, 1, count) for member in segments], offsets)
    lists = lax.all_gather(lists, "seg")
    side, own, meta = call(
        first_kernel,
        "first",
        (shaped(4 * COLS, BLOCK, dtype=BF16), shaped(4 * COLS, BLOCK), shaped(32, BLOCK, dtype=BF16)),
        (VMEM, VMEM, VMEM),
        [
            pltpu.VMEM((8, rows), F32),
            pltpu.VMEM((8, rows), F32),
            pltpu.VMEM((BLOCK, BLOCK), BF16),
            pltpu.VMEM((2, 4, COLS, BLOCK), F32),
        ],
    )(lists, density.T, marks)
    sides = gather(side, axis_index_groups=pair_groups(boxes))
    came = jnp.where(ahead == 1, sides[1], sides[0])
    mixed = (own + came.astype(F32)).astype(BF16)
    parts = gather(jnp.concatenate([mixed, meta], axis=0), axis_index_groups=half_groups(boxes))
    density_one, side, own = call(
        second_kernel,
        "second",
        (shaped(COLS, rows, dtype=BF16), shaped(2 * COLS, BLOCK, dtype=BF16), shaped(2 * COLS, BLOCK)),
        (ANY, VMEM, VMEM),
        [
            pltpu.VMEM((COLS, rows), BF16),
            pltpu.VMEM((2, 8, rows), F32),
            pltpu.VMEM((2, 8, rows), F32),
            pltpu.VMEM((4, COLS, BLOCK), BF16),
            pltpu.VMEM((BLOCK, BLOCK), BF16),
            pltpu.VMEM((2, 2, COLS, BLOCK), F32),
            pltpu.SemaphoreType.DMA,
        ],
    )(parts)
    sides = gather(side, axis_index_groups=pair_groups(boxes))
    came = jnp.where(ahead == 1, sides[1], sides[0])
    both = gather(own + came.astype(F32), axis_index_groups=core_groups(boxes))
    density_two = call(
        last_kernel,
        "last",
        shaped(COLS, rows, dtype=BF16),
        ANY,
        [pltpu.VMEM((COLS, rows), BF16), pltpu.SemaphoreType.DMA],
    )(both)
    return density_one.T, density_two.T


def solution(mesh):
    boxed = P("box", None)
    lined = P("box", "seg", None)
    return jax.shard_map(
        body,
        mesh=mesh,
        in_specs=(boxed, boxed) + (lined,) * 8,
        out_specs=(boxed, boxed),
        check_vma=False,
    )
```

```python
import functools

import jax
import jax.numpy as jnp
from jax import lax
from jax.experimental import pallas as pl
from jax.experimental.pallas import tpu as pltpu
from jax.sharding import PartitionSpec as P

F32 = jnp.float32
BF16 = jnp.bfloat16
BLOCK = 256
COLS = 64
WIDTH = 4
GROUP = 4
AXES = ("box", "seg")


def place():
    box = lax.axis_index("box")
    core = lax.axis_index("seg") % 2
    pair = box // 2
    return pair, box % 2, core, 1 - (pair + core) % 2


def pair_groups(boxes):
    pairs = boxes // 2
    groups = []
    for first in range(pairs):
        second = (first + 1) % pairs
        for chip in range(4):
            core = first % 2
            groups.append([first * 8 + chip * 2 + core, second * 8 + chip * 2 + core])
    return groups


def core_groups(boxes):
    return [[2 * chip, 2 * chip + 1] for chip in range(boxes * 2)]


def half_groups(boxes):
    groups = []
    for pair in range(boxes // 2):
        groups.append([pair * 8 + i for i in (2, 3, 4, 5)])
        groups.append([pair * 8 + i for i in (0, 1, 6, 7)])
    return groups


def iota(shape, dim):
    return lax.broadcasted_iota(jnp.int32, shape, dim)


def across(left, right):
    return lax.dot_general(left, right, (((1,), (1,)), ((), ())), preferred_element_type=F32)


def sort_kernel(*refs):
    *ins, offsets_ref, out_ref, marks_ref = refs
    offs = offsets_ref[...].astype(F32)
    marks_ref[...] = jnp.concatenate(
        [jnp.broadcast_to(offs[j : j + 1, s : s + 1], (1, 128)) for j in range(2) for s in range(WIDTH)], axis=0
    )
    chunks = ins[0].shape[0]
    past = float(128 * chunks)
    below = iota((8, 128), 0).astype(F32)
    wants = [(iota((8, 128), 1) + 128 * q).astype(F32) for q in range(4)]
    for day in range(2):
        start, slot, end, weight = (ref[...] for ref in ins[4 * day : 4 * day + 4])
        turned = start.astype(F32).T
        firsts = [jnp.full((8, 128), past, F32)] * 4
        lasts = [jnp.full((8, 128), -1.0, F32)] * 4
        for c in range(chunks):
            wide = jnp.broadcast_to(turned[:, c : c + 1], (128, 128))
            for i in range(16):
                at = below + float(128 * c + 8 * i)
                for q in range(4):
                    hit = wide[8 * i : 8 * i + 8] == wants[q]
                    firsts[q] = jnp.minimum(firsts[q], jnp.where(hit, at, past))
                    lasts[q] = jnp.where(hit, at, lasts[q])
        firsts = [jnp.min(one, axis=0, keepdims=True) for one in firsts]
        lasts = [jnp.max(one, axis=0, keepdims=True) for one in lasts]
        spots = jnp.concatenate(firsts + lasts, axis=0)
        chunk = jnp.floor(spots * (1.0 / 128))
        lane = (spots - chunk * 128.0).astype(jnp.int32)
        for field, values in enumerate((slot.astype(F32) * float(BLOCK) + end.astype(F32), weight)):
            got = None
            for c in range(chunks):
                row = jnp.broadcast_to(values[c : c + 1], (8, 128))
                part = jnp.take_along_axis(row, lane, axis=1, mode="promise_in_bounds")
                got = part if got is None else jnp.where(chunk == float(c), part, got)
            at = 16 * day + 8 * field
            out_ref[at : at + 8, :] = got


def split_work(blocks, half_only, ahead):
    places = []
    for block in blocks:
        place_of = jnp.where(block < 0, 0, jnp.where(block >= 4, 1, 2))
        if half_only is not None:
            place_of = jnp.where(((block >> 1) & 1) == half_only, place_of, 3)
        places.append(place_of)
    behind, front, inside = (sum((p == kind).astype(jnp.int32) for p in places) for kind in range(3))
    share = jnp.clip(((behind + front + inside + 1) >> 1) - front, 0, inside)
    mine, seen = [], 0
    for p in places:
        is_inside = p == 2
        taker = jnp.where(seen < share, 1, 0)
        mine.append(jnp.logical_or(p == ahead, jnp.logical_and(is_inside, taker == ahead)))
        seen = seen + is_inside.astype(jnp.int32)
    return places, mine


def fold(tiles, part):
    low = (iota((8, 128), 0) & 3) < 2
    one, two = tiles
    return jnp.where(
        low,
        jnp.where(part == 0, one, pltpu.roll(one, 6, 0)),
        jnp.where(part == 0, pltpu.roll(two, 2, 0), two),
    )


def list_work(work_ref, blocks, places, mine, spots):
    done = jnp.int32(0)
    for number, (block, place_of, take) in enumerate(zip(blocks, places, mine)):
        at = jnp.where(place_of == 2, spots, 0) + (block & (spots - 1))
        work_ref[done] = number * 16 + at
        done = done + take.astype(jnp.int32)
    for i in range(GROUP):
        work_ref[done + i] = 2 * spots
    return done


def push_blocks(work_ref, done, key_ref, weight_ref, from_ref, counts_ref, sums_ref):
    step = 16
    first = iota((step, BLOCK), 0).astype(F32)
    zero = jnp.zeros((step, BLOCK), BF16)

    @pl.loop(0, (done + GROUP - 1) // GROUP)
    def _(group):
        items = [work_ref[group * GROUP + i] for i in range(GROUP)]
        for i, item in enumerate(items):
            j = item >> 6
            base = (((item >> 4) & 3) * BLOCK).astype(F32)
            keys, weights = [], []
            for side in range(2):
                key_tile = key_ref[2 * j + side] - base
                weight_tile = weight_ref[2 * j + side]
                for row in (0, 2, 4, 6):
                    two = [slice(row + t, row + t + 1) for t in range(2)]
                    wide = [
                        jnp.concatenate([jnp.broadcast_to(tile[one, :], (step, 128)) for one in two], axis=1).astype(BF16)
                        for tile in (key_tile, weight_tile)
                    ]
                    keys.append(wide[0])
                    weights.append(wide[1])
            for at in range(0, BLOCK, step):
                ends = (first + float(at)).astype(BF16)
                total = None
                for key, weight in zip(keys, weights):
                    term = jnp.where(key == ends, weight, zero)
                    total = term if total is None else total + term
                counts_ref[i, at : at + step, :] = total
        pushed = [across(from_ref[item >> 6], counts_ref[i]) for i, item in enumerate(items)]
        for item, one in zip(items, pushed):
            sums_ref[item & 15] += one


def first_kernel(lists_ref, density_ref, marks_ref, side_ref, own_ref, meta_ref, key_ref, weight_ref, from_ref, counts_ref, sums_ref, work_ref):
    pair, half, core, ahead = place()
    lanes = lists_ref.shape[0]
    marks = marks_ref[...]
    whole = marks.astype(jnp.int32)
    blocks = [2 * half + i // WIDTH + whole[i, 0] for i in range(2 * WIDTH)]
    places, mine = split_work(blocks, None, ahead)
    done = list_work(work_ref, blocks, places, mine, 4)
    for j in range(2):
        from_ref[j] = density_ref[:, BLOCK * j : BLOCK * j + BLOCK]
    for day in range(2):
        keys = [lists_ref[lane, 16 * day : 16 * day + 8, :] for lane in range(lanes)]
        weights = [lists_ref[lane, 16 * day + 8 : 16 * day + 16, :] for lane in range(lanes)]
        total = weights[0] + weights[1] + weights[2] + weights[3]
        total = total + pltpu.roll(total, 4, 0)
        weights = [weight / total for weight in weights]
        if day == 0:
            for j in range(2):
                for side in range(2):
                    key_ref[2 * j + side] = fold(keys[2 * side : 2 * side + 2], j)
                    weight_ref[2 * j + side] = fold(weights[2 * side : 2 * side + 2], j)
        else:
            slots = [jnp.floor(key * (1.0 / BLOCK)) for key in keys]
            ends = [key - slot * float(BLOCK) for key, slot in zip(keys, slots)]
            pieces = [
                jnp.concatenate([fold(field[:2], core), fold(field[2:], core)], axis=1) for field in (ends, slots, weights)
            ]
            meta_ref[...] = jnp.concatenate(pieces + [jnp.concatenate([marks, marks], axis=1)], axis=0).astype(BF16)
    sums_ref[...] = jnp.zeros_like(sums_ref)
    push_blocks(work_ref, done, key_ref, weight_ref, from_ref, counts_ref, sums_ref)
    for spot in range(4):
        cut = slice(COLS * spot, COLS * spot + COLS)
        side_ref[cut, :] = sums_ref[spot].astype(BF16)
        own_ref[cut, :] = sums_ref[4 + spot]


def second_kernel(parts_ref, density_ref, side_ref, own_ref, stage_ref, key_ref, weight_ref, from_ref, counts_ref, sums_ref, work_ref, sem):
    pair, half, core, ahead = place()
    wide = 4 * COLS
    blocks = []
    for j in range(4):
        piece = parts_ref[j, wide : wide + 32, :].astype(F32)
        keys = piece[8:16] * float(BLOCK) + piece[0:8]
        for side in range(2):
            cut = slice(128 * side, 128 * side + 128)
            key_ref[2 * j + side] = keys[:, cut]
            weight_ref[2 * j + side] = piece[16:24, cut]
        whole = piece[24:32, :128].astype(jnp.int32)
        blocks += [j + whole[WIDTH * (j & 1) + s, 0] for s in range(WIDTH)]
    places, mine = split_work(blocks, half, ahead)
    done = list_work(work_ref, blocks, places, mine, 2)
    for j in range(4):
        cut = slice(COLS * j, COLS * j + COLS)
        one, two, three, four = (parts_ref[i, cut, :].astype(F32) for i in range(4))
        from_ref[j] = ((one + two) + (three + four)).astype(BF16)
    for part in range(2):
        stage_ref[:, BLOCK * part : BLOCK * part + BLOCK] = from_ref[2 * half + part]
    store = pltpu.make_async_copy(stage_ref, density_ref, sem)
    store.start()
    sums_ref[...] = jnp.zeros_like(sums_ref)
    push_blocks(work_ref, done, key_ref, weight_ref, from_ref, counts_ref, sums_ref)
    for spot in range(2):
        cut = slice(COLS * spot, COLS * spot + COLS)
        side_ref[cut, :] = sums_ref[spot].astype(BF16)
        own_ref[cut, :] = sums_ref[2 + spot]
    store.wait()


def last_kernel(both_ref, density_ref, stage_ref, sem):
    total = (both_ref[0] + both_ref[1]).astype(BF16)
    stage_ref[:, :BLOCK] = total[:COLS]
    stage_ref[:, BLOCK:] = total[COLS:]
    store = pltpu.make_async_copy(stage_ref, density_ref, sem)
    store.start()
    store.wait()


VMEM = pl.BlockSpec(memory_space=pltpu.VMEM)
ANY = pl.BlockSpec(memory_space=pl.ANY)


def call(kernel, name, outs, out_specs, scratch):
    return pl.pallas_call(
        kernel,
        out_shape=outs,
        out_specs=out_specs,
        scratch_shapes=scratch,
        compiler_params=pltpu.CompilerParams(vmem_limit_bytes=32 * 1024 * 1024),
        name=name,
    )


def shaped(*shape, dtype=F32):
    return jax.ShapeDtypeStruct(shape, dtype)


def body(density, offsets, *segments):
    boxes = lax.axis_size("box")
    rows = density.shape[0]
    count = segments[0].shape[-1]
    gather = functools.partial(lax.all_gather, axis_name=AXES)
    pair, half, core, ahead = place()

    lists, marks = call(
        sort_kernel,
        "sort",
        (shaped(32, 128), shaped(8, 128)),
        (VMEM, VMEM),
        [],
    )(*[member.reshape(count // 128, 128) for member in segments], offsets)
    lists = lax.all_gather(lists, "seg")
    side, own, meta = call(
        first_kernel,
        "first",
        (shaped(4 * COLS, BLOCK, dtype=BF16), shaped(4 * COLS, BLOCK), shaped(32, BLOCK, dtype=BF16)),
        (VMEM, VMEM, VMEM),
        [
            pltpu.VMEM((4, 8, 128), F32),
            pltpu.VMEM((4, 8, 128), F32),
            pltpu.VMEM((2, COLS, BLOCK), BF16),
            pltpu.VMEM((GROUP, BLOCK, BLOCK), BF16),
            pltpu.VMEM((9, COLS, BLOCK), F32),
            pltpu.SMEM((2 * WIDTH + GROUP,), jnp.int32),
        ],
    )(lists, density.T, marks)
    sides = gather(side, axis_index_groups=pair_groups(boxes))
    came = jnp.where(ahead == 1, sides[1], sides[0])
    mixed = (own + came.astype(F32)).astype(BF16)
    parts = gather(jnp.concatenate([mixed, meta], axis=0), axis_index_groups=half_groups(boxes))
    density_one, side, own = call(
        second_kernel,
        "second",
        (shaped(COLS, rows, dtype=BF16), shaped(2 * COLS, BLOCK, dtype=BF16), shaped(2 * COLS, BLOCK)),
        (ANY, VMEM, VMEM),
        [
            pltpu.VMEM((COLS, rows), BF16),
            pltpu.VMEM((8, 8, 128), F32),
            pltpu.VMEM((8, 8, 128), F32),
            pltpu.VMEM((4, COLS, BLOCK), BF16),
            pltpu.VMEM((GROUP, BLOCK, BLOCK), BF16),
            pltpu.VMEM((5, COLS, BLOCK), F32),
            pltpu.SMEM((4 * WIDTH + GROUP,), jnp.int32),
            pltpu.SemaphoreType.DMA,
        ],
    )(parts)
    sides = gather(side, axis_index_groups=pair_groups(boxes))
    came = jnp.where(ahead == 1, sides[1], sides[0])
    both = gather(own + came.astype(F32), axis_index_groups=core_groups(boxes))
    density_two = call(
        last_kernel,
        "last",
        shaped(COLS, rows, dtype=BF16),
        ANY,
        [pltpu.VMEM((COLS, rows), BF16), pltpu.SemaphoreType.DMA],
    )(both)
    return density_one.T, density_two.T


def solution(mesh):
    boxed = P("box", None)
    lined = P("box", "seg", None)
    return jax.shard_map(
        body,
        mesh=mesh,
        in_specs=(boxed, boxed) + (lined,) * 8,
        out_specs=(boxed, boxed),
        check_vma=False,
    )
```

```python
import functools

import jax
import jax.numpy as jnp
from jax import lax
from jax.experimental import pallas as pl
from jax.experimental.pallas import tpu as pltpu
from jax.sharding import PartitionSpec as P

F32 = jnp.float32
BF16 = jnp.bfloat16
BLOCK = 256
COLS = 64
WIDTH = 4
GROUPS = (4, 5)
AXES = ("box", "seg")


def place():
    box = lax.axis_index("box")
    core = lax.axis_index("seg") % 2
    pair = box // 2
    return pair, box % 2, core, 1 - (pair + core) % 2


def pair_groups(boxes):
    pairs = boxes // 2
    groups = []
    for first in range(pairs):
        second = (first + 1) % pairs
        for chip in range(4):
            core = first % 2
            groups.append([first * 8 + chip * 2 + core, second * 8 + chip * 2 + core])
    return groups


def core_groups(boxes):
    return [[2 * chip, 2 * chip + 1] for chip in range(boxes * 2)]


def half_groups(boxes):
    groups = []
    for pair in range(boxes // 2):
        groups.append([pair * 8 + i for i in (2, 3, 4, 5)])
        groups.append([pair * 8 + i for i in (0, 1, 6, 7)])
    return groups


def iota(shape, dim):
    return lax.broadcasted_iota(jnp.int32, shape, dim)


def across(left, right):
    return lax.dot_general(left, right, (((1,), (1,)), ((), ())), preferred_element_type=F32)


def sort_kernel(*refs):
    *ins, offsets_ref, out_ref, marks_ref = refs
    offs = offsets_ref[...].astype(F32)
    marks_ref[...] = jnp.concatenate(
        [jnp.broadcast_to(offs[j : j + 1, s : s + 1], (1, 128)) for j in range(2) for s in range(WIDTH)], axis=0
    )
    chunks = ins[0].shape[0]
    past = float(128 * chunks)
    below = iota((8, 128), 0).astype(F32)
    wants = [(iota((8, 128), 1) + 128 * q).astype(F32) for q in range(4)]
    found = []
    for day in range(2):
        start, slot, end, weight = (ref[...] for ref in ins[4 * day : 4 * day + 4])
        turned = start.astype(F32).T
        firsts = [jnp.full((8, 128), past, F32)] * 4
        lasts = [jnp.full((8, 128), -1.0, F32)] * 4
        for c in range(chunks):
            wide = jnp.broadcast_to(turned[:, c : c + 1], (128, 128))
            for i in range(16):
                at = below + float(128 * c + 8 * i)
                for q in range(4):
                    hit = wide[8 * i : 8 * i + 8] == wants[q]
                    firsts[q] = jnp.minimum(firsts[q], jnp.where(hit, at, past))
                    lasts[q] = jnp.where(hit, at, lasts[q])
        firsts = [jnp.min(one, axis=0, keepdims=True) for one in firsts]
        lasts = [jnp.max(one, axis=0, keepdims=True) for one in lasts]
        spots = jnp.concatenate(firsts + lasts, axis=0)
        chunk = jnp.floor(spots * (1.0 / 128))
        lane = (spots - chunk * 128.0).astype(jnp.int32)
        for values in (end.astype(F32), slot.astype(F32), weight):
            got = None
            for c in range(chunks):
                row = jnp.broadcast_to(values[c : c + 1], (8, 128))
                part = jnp.take_along_axis(row, lane, axis=1, mode="promise_in_bounds")
                got = part if got is None else jnp.where(chunk == float(c), part, got)
            found.append(got)
    out_ref[...] = jnp.concatenate(found, axis=0).astype(BF16)


def split_work(blocks, half_only, ahead):
    places = []
    for block in blocks:
        place_of = jnp.where(block < 0, 0, jnp.where(block >= 4, 1, 2))
        if half_only is not None:
            place_of = jnp.where(((block >> 1) & 1) == half_only, place_of, 3)
        places.append(place_of)
    behind, front, inside = (sum((p == kind).astype(jnp.int32) for p in places) for kind in range(3))
    share = jnp.clip(((behind + front + inside + 1) >> 1) - front, 0, inside)
    mine, seen = [], 0
    for p in places:
        is_inside = p == 2
        taker = jnp.where(seen < share, 1, 0)
        mine.append(jnp.logical_or(p == ahead, jnp.logical_and(is_inside, taker == ahead)))
        seen = seen + is_inside.astype(jnp.int32)
    return places, mine


def fold(tiles, part):
    low = (iota((8, 128), 0) & 3) < 2
    one, two = tiles
    return jnp.where(
        low,
        jnp.where(part == 0, one, pltpu.roll(one, 6, 0)),
        jnp.where(part == 0, pltpu.roll(two, 2, 0), two),
    )


def list_work(work_ref, blocks, places, mine, spots, size):
    done = jnp.int32(0)
    for number, (block, place_of, take) in enumerate(zip(blocks, places, mine)):
        at = jnp.where(place_of == 2, spots, 0) + (block & (spots - 1))
        work_ref[done] = number * 16 + at
        done = done + take.astype(jnp.int32)
    for i in range(size):
        work_ref[done + i] = 2 * spots
    return done


def push_blocks(work_ref, done, key_ref, weight_ref, from_ref, counts_ref, sums_ref):
    step = 16
    first = iota((step, BLOCK), 0).astype(F32)
    zero = jnp.zeros((step, BLOCK), BF16)

    size = counts_ref.shape[0]

    @pl.loop(0, (done + size - 1) // size)
    def _(group):
        items = [work_ref[group * size + i] for i in range(size)]
        for i, item in enumerate(items):
            j = item >> 6
            base = (((item >> 4) & 3) * BLOCK).astype(F32)
            keys, weights = [], []
            for side in range(2):
                key_tile = key_ref[2 * j + side] - base
                weight_tile = weight_ref[2 * j + side]
                for row in (0, 2, 4, 6):
                    two = [slice(row + t, row + t + 1) for t in range(2)]
                    wide = [
                        jnp.concatenate([jnp.broadcast_to(tile[one, :], (step, 128)) for one in two], axis=1).astype(BF16)
                        for tile in (key_tile, weight_tile)
                    ]
                    keys.append(wide[0])
                    weights.append(wide[1])
            for at in range(0, BLOCK, step):
                ends = (first + float(at)).astype(BF16)
                total = None
                for key, weight in zip(keys, weights):
                    term = jnp.where(key == ends, weight, zero)
                    total = term if total is None else total + term
                counts_ref[i, at : at + step, :] = total
        pushed = [across(from_ref[item >> 6], counts_ref[i]) for i, item in enumerate(items)]
        for item, one in zip(items, pushed):
            sums_ref[item & 15] += one


def first_kernel(lists_ref, density_ref, marks_ref, side_ref, own_ref, meta_ref, key_ref, weight_ref, from_ref, counts_ref, sums_ref, work_ref):
    pair, half, core, ahead = place()
    lanes = lists_ref.shape[0]
    marks = marks_ref[...]
    whole = marks.astype(jnp.int32)
    blocks = [2 * half + i // WIDTH + whole[i, 0] for i in range(2 * WIDTH)]
    places, mine = split_work(blocks, None, ahead)
    done = list_work(work_ref, blocks, places, mine, 4, counts_ref.shape[0])
    for j in range(2):
        from_ref[j] = density_ref[:, BLOCK * j : BLOCK * j + BLOCK]
    lists = [lists_ref[lane].astype(F32) for lane in range(lanes)]
    for day in range(2):
        ends, slots, weights = (
            [one[24 * day + 8 * field : 24 * day + 8 * field + 8] for one in lists] for field in range(3)
        )
        total = weights[0] + weights[1] + weights[2] + weights[3]
        total = total + pltpu.roll(total, 4, 0)
        weights = [weight / total for weight in weights]
        if day == 0:
            keys = [slot * float(BLOCK) + end for slot, end in zip(slots, ends)]
            for j in range(2):
                for side in range(2):
                    key_ref[2 * j + side] = fold(keys[2 * side : 2 * side + 2], j)
                    weight_ref[2 * j + side] = fold(weights[2 * side : 2 * side + 2], j)
        else:
            pieces = [
                jnp.concatenate([fold(field[:2], core), fold(field[2:], core)], axis=1) for field in (ends, slots, weights)
            ]
            meta_ref[...] = jnp.concatenate(pieces + [jnp.concatenate([marks, marks], axis=1)], axis=0).astype(BF16)
    sums_ref[...] = jnp.zeros_like(sums_ref)
    push_blocks(work_ref, done, key_ref, weight_ref, from_ref, counts_ref, sums_ref)
    for spot in range(4):
        cut = slice(COLS * spot, COLS * spot + COLS)
        side_ref[cut, :] = sums_ref[spot].astype(BF16)
        own_ref[cut, :] = sums_ref[4 + spot]


def second_kernel(parts_ref, density_ref, side_ref, own_ref, stage_ref, key_ref, weight_ref, from_ref, counts_ref, sums_ref, work_ref, sem):
    pair, half, core, ahead = place()
    wide = 4 * COLS
    blocks = []
    for j in range(4):
        piece = parts_ref[j, wide : wide + 32, :].astype(F32)
        keys = piece[8:16] * float(BLOCK) + piece[0:8]
        for side in range(2):
            cut = slice(128 * side, 128 * side + 128)
            key_ref[2 * j + side] = keys[:, cut]
            weight_ref[2 * j + side] = piece[16:24, cut]
        whole = piece[24:32, :128].astype(jnp.int32)
        blocks += [j + whole[WIDTH * (j & 1) + s, 0] for s in range(WIDTH)]
    places, mine = split_work(blocks, half, ahead)
    done = list_work(work_ref, blocks, places, mine, 2, counts_ref.shape[0])
    for j in range(4):
        cut = slice(COLS * j, COLS * j + COLS)
        one, two, three, four = (parts_ref[i, cut, :].astype(F32) for i in range(4))
        from_ref[j] = ((one + two) + (three + four)).astype(BF16)
    for part in range(2):
        stage_ref[:, BLOCK * part : BLOCK * part + BLOCK] = from_ref[2 * half + part]
    store = pltpu.make_async_copy(stage_ref, density_ref, sem)
    store.start()
    sums_ref[...] = jnp.zeros_like(sums_ref)
    push_blocks(work_ref, done, key_ref, weight_ref, from_ref, counts_ref, sums_ref)
    for spot in range(2):
        cut = slice(COLS * spot, COLS * spot + COLS)
        side_ref[cut, :] = sums_ref[spot].astype(BF16)
        own_ref[cut, :] = sums_ref[2 + spot]
    store.wait()


def last_kernel(both_ref, density_ref, stage_ref, sem):
    total = (both_ref[0].astype(F32) + both_ref[1].astype(F32)).astype(BF16)
    stage_ref[:, :BLOCK] = total[:COLS]
    stage_ref[:, BLOCK:] = total[COLS:]
    store = pltpu.make_async_copy(stage_ref, density_ref, sem)
    store.start()
    store.wait()


VMEM = pl.BlockSpec(memory_space=pltpu.VMEM)
ANY = pl.BlockSpec(memory_space=pl.ANY)


def call(kernel, name, outs, out_specs, scratch):
    return pl.pallas_call(
        kernel,
        out_shape=outs,
        out_specs=out_specs,
        scratch_shapes=scratch,
        compiler_params=pltpu.CompilerParams(vmem_limit_bytes=32 * 1024 * 1024),
        name=name,
    )


def shaped(*shape, dtype=F32):
    return jax.ShapeDtypeStruct(shape, dtype)


def body(density, offsets, *segments):
    boxes = lax.axis_size("box")
    rows = density.shape[0]
    count = segments[0].shape[-1]
    gather = functools.partial(lax.all_gather, axis_name=AXES)
    pair, half, core, ahead = place()

    lists, marks = call(
        sort_kernel,
        "sort",
        (shaped(48, 128, dtype=BF16), shaped(8, 128)),
        (VMEM, VMEM),
        [],
    )(*[member.reshape(count // 128, 128) for member in segments], offsets)
    lists = lax.all_gather(lists, "seg")
    side, own, meta = call(
        first_kernel,
        "first",
        (shaped(4 * COLS, BLOCK, dtype=BF16), shaped(4 * COLS, BLOCK), shaped(32, BLOCK, dtype=BF16)),
        (VMEM, VMEM, VMEM),
        [
            pltpu.VMEM((4, 8, 128), F32),
            pltpu.VMEM((4, 8, 128), F32),
            pltpu.VMEM((2, COLS, BLOCK), BF16),
            pltpu.VMEM((GROUPS[0], BLOCK, BLOCK), BF16),
            pltpu.VMEM((9, COLS, BLOCK), F32),
            pltpu.SMEM((2 * WIDTH + GROUPS[0],), jnp.int32),
        ],
    )(lists, density.T, marks)
    sides = gather(side, axis_index_groups=pair_groups(boxes))
    came = jnp.where(ahead == 1, sides[1], sides[0])
    mixed = (own + came.astype(F32)).astype(BF16)
    parts = gather(jnp.concatenate([mixed, meta], axis=0), axis_index_groups=half_groups(boxes))
    density_one, side, own = call(
        second_kernel,
        "second",
        (shaped(COLS, rows, dtype=BF16), shaped(2 * COLS, BLOCK, dtype=BF16), shaped(2 * COLS, BLOCK)),
        (ANY, VMEM, VMEM),
        [
            pltpu.VMEM((COLS, rows), BF16),
            pltpu.VMEM((8, 8, 128), F32),
            pltpu.VMEM((8, 8, 128), F32),
            pltpu.VMEM((4, COLS, BLOCK), BF16),
            pltpu.VMEM((GROUPS[1], BLOCK, BLOCK), BF16),
            pltpu.VMEM((5, COLS, BLOCK), F32),
            pltpu.SMEM((4 * WIDTH + GROUPS[1],), jnp.int32),
            pltpu.SemaphoreType.DMA,
        ],
    )(parts)
    sides = gather(side, axis_index_groups=pair_groups(boxes))
    came = jnp.where(ahead == 1, sides[1], sides[0])
    both = gather((own + came.astype(F32)).astype(BF16), axis_index_groups=core_groups(boxes))
    density_two = call(
        last_kernel,
        "last",
        shaped(COLS, rows, dtype=BF16),
        ANY,
        [pltpu.VMEM((COLS, rows), BF16), pltpu.SemaphoreType.DMA],
    )(both)
    return density_one.T, density_two.T


def solution(mesh):
    boxed = P("box", None)
    lined = P("box", "seg", None)
    return jax.shard_map(
        body,
        mesh=mesh,
        in_specs=(boxed, boxed) + (lined,) * 8,
        out_specs=(boxed, boxed),
        check_vma=False,
    )
```

```python
import functools

import jax
import jax.numpy as jnp
from jax import lax
from jax.experimental import pallas as pl
from jax.experimental.pallas import tpu as pltpu
from jax.sharding import PartitionSpec as P

F32 = jnp.float32
BF16 = jnp.bfloat16
BLOCK = 256
COLS = 64
WIDTH = 4
GROUP = 4
AXES = ("box", "seg")


def place():
    box = lax.axis_index("box")
    core = lax.axis_index("seg") % 2
    pair = box // 2
    return pair, box % 2, core, 1 - (pair + core) % 2


def pair_groups(boxes):
    pairs = boxes // 2
    groups = []
    for first in range(pairs):
        second = (first + 1) % pairs
        for chip in range(4):
            core = first % 2
            groups.append([first * 8 + chip * 2 + core, second * 8 + chip * 2 + core])
    return groups


def core_groups(boxes):
    return [[2 * chip, 2 * chip + 1] for chip in range(boxes * 2)]


def half_groups(boxes):
    groups = []
    for pair in range(boxes // 2):
        groups.append([pair * 8 + i for i in (2, 3, 4, 5)])
        groups.append([pair * 8 + i for i in (0, 1, 6, 7)])
    return groups


def iota(shape, dim):
    return lax.broadcasted_iota(jnp.int32, shape, dim)


def across(left, right):
    return lax.dot_general(left, right, (((1,), (1,)), ((), ())), preferred_element_type=F32)


def sort_kernel(*refs):
    *ins, offsets_ref, out_ref, marks_ref = refs
    offs = offsets_ref[...].astype(F32)
    marks_ref[...] = jnp.concatenate(
        [jnp.broadcast_to(offs[j : j + 1, s : s + 1], (1, 128)) for j in range(2) for s in range(WIDTH)], axis=0
    )
    chunks = ins[0].shape[0]
    past = float(128 * chunks)
    below = iota((8, 128), 0).astype(F32)
    wants = [(iota((8, 128), 1) + 128 * q).astype(F32) for q in range(4)]
    for day in range(2):
        start, slot, end, weight = (ref[...] for ref in ins[4 * day : 4 * day + 4])
        turned = start.astype(F32).T
        firsts = [jnp.full((8, 128), past, F32)] * 4
        lasts = [jnp.full((8, 128), -1.0, F32)] * 4
        for c in range(chunks):
            wide = jnp.broadcast_to(turned[:, c : c + 1], (128, 128))
            for i in range(16):
                at = below + float(128 * c + 8 * i)
                for q in range(4):
                    hit = wide[8 * i : 8 * i + 8] == wants[q]
                    firsts[q] = jnp.minimum(firsts[q], jnp.where(hit, at, past))
                    lasts[q] = jnp.where(hit, at, lasts[q])
        firsts = [jnp.min(one, axis=0, keepdims=True) for one in firsts]
        lasts = [jnp.max(one, axis=0, keepdims=True) for one in lasts]
        spots = jnp.concatenate(firsts + lasts, axis=0)
        chunk = jnp.floor(spots * (1.0 / 128))
        lane = (spots - chunk * 128.0).astype(jnp.int32)
        for field, values in enumerate((slot.astype(F32) * float(BLOCK) + end.astype(F32), weight)):
            got = None
            for c in range(chunks):
                row = jnp.broadcast_to(values[c : c + 1], (8, 128))
                part = jnp.take_along_axis(row, lane, axis=1, mode="promise_in_bounds")
                got = part if got is None else jnp.where(chunk == float(c), part, got)
            at = 16 * day + 8 * field
            out_ref[at : at + 8, :] = got


def split_work(blocks, half_only, ahead):
    places = []
    for block in blocks:
        place_of = jnp.where(block < 0, 0, jnp.where(block >= 4, 1, 2))
        if half_only is not None:
            place_of = jnp.where(((block >> 1) & 1) == half_only, place_of, 3)
        places.append(place_of)
    behind, front, inside = (sum((p == kind).astype(jnp.int32) for p in places) for kind in range(3))
    share = jnp.clip(((behind + front + inside + 1) >> 1) - front, 0, inside)
    mine, seen = [], 0
    for p in places:
        is_inside = p == 2
        taker = jnp.where(seen < share, 1, 0)
        mine.append(jnp.logical_or(p == ahead, jnp.logical_and(is_inside, taker == ahead)))
        seen = seen + is_inside.astype(jnp.int32)
    return places, mine


def fold(tiles, part):
    low = (iota((8, 128), 0) & 3) < 2
    one, two = tiles
    return jnp.where(
        low,
        jnp.where(part == 0, one, pltpu.roll(one, 6, 0)),
        jnp.where(part == 0, pltpu.roll(two, 2, 0), two),
    )


def list_work(work_ref, blocks, places, mine, spots):
    done = jnp.int32(0)
    for number, (block, place_of, take) in enumerate(zip(blocks, places, mine)):
        at = jnp.where(place_of == 2, spots, 0) + (block & (spots - 1))
        work_ref[done] = number * 16 + at
        done = done + take.astype(jnp.int32)
    for i in range(GROUP):
        work_ref[done + i] = 2 * spots
    return done


def push_blocks(work_ref, done, key_ref, weight_ref, from_ref, counts_ref, sums_ref):
    step = 16
    first = iota((step, BLOCK), 0).astype(F32)
    zero = jnp.zeros((step, BLOCK), BF16)

    @pl.loop(0, (done + GROUP - 1) // GROUP)
    def _(group):
        items = [work_ref[group * GROUP + i] for i in range(GROUP)]
        for i, item in enumerate(items):
            j = item >> 6
            base = (((item >> 4) & 3) * BLOCK).astype(F32)
            keys, weights = [], []
            for side in range(2):
                key_tile = key_ref[2 * j + side] - base
                weight_tile = weight_ref[2 * j + side]
                for row in (0, 2, 4, 6):
                    two = [slice(row + t, row + t + 1) for t in range(2)]
                    wide = [
                        jnp.concatenate([jnp.broadcast_to(tile[one, :], (step, 128)) for one in two], axis=1).astype(BF16)
                        for tile in (key_tile, weight_tile)
                    ]
                    keys.append(wide[0])
                    weights.append(wide[1])
            for at in range(0, BLOCK, step):
                ends = (first + float(at)).astype(BF16)
                total = None
                for key, weight in zip(keys, weights):
                    term = jnp.where(key == ends, weight, zero)
                    total = term if total is None else total + term
                counts_ref[i, at : at + step, :] = total
        pushed = [across(from_ref[item >> 6], counts_ref[i]) for i, item in enumerate(items)]
        for item, one in zip(items, pushed):
            sums_ref[item & 15] += one


def first_kernel(lists_ref, density_ref, marks_ref, side_ref, own_ref, meta_ref, key_ref, weight_ref, from_ref, counts_ref, sums_ref, work_ref):
    pair, half, core, ahead = place()
    lanes = lists_ref.shape[0]
    marks = marks_ref[...]
    whole = marks.astype(jnp.int32)
    blocks = [2 * half + i // WIDTH + whole[i, 0] for i in range(2 * WIDTH)]
    places, mine = split_work(blocks, None, ahead)
    done = list_work(work_ref, blocks, places, mine, 4)
    for j in range(2):
        from_ref[j] = density_ref[:, BLOCK * j : BLOCK * j + BLOCK]
    for day in range(2):
        keys = [lists_ref[lane, 16 * day : 16 * day + 8, :] for lane in range(lanes)]
        weights = [lists_ref[lane, 16 * day + 8 : 16 * day + 16, :] for lane in range(lanes)]
        total = weights[0] + weights[1] + weights[2] + weights[3]
        total = total + pltpu.roll(total, 4, 0)
        weights = [weight / total for weight in weights]
        if day == 0:
            for j in range(2):
                for side in range(2):
                    key_ref[2 * j + side] = fold(keys[2 * side : 2 * side + 2], j)
                    weight_ref[2 * j + side] = fold(weights[2 * side : 2 * side + 2], j)
        else:
            slots = [jnp.floor(key * (1.0 / BLOCK)) for key in keys]
            ends = [key - slot * float(BLOCK) for key, slot in zip(keys, slots)]
            pieces = [
                jnp.concatenate([fold(field[:2], core), fold(field[2:], core)], axis=1) for field in (ends, slots, weights)
            ]
            meta_ref[...] = jnp.concatenate(pieces + [jnp.concatenate([marks, marks], axis=1)], axis=0).astype(BF16)
    sums_ref[...] = jnp.zeros_like(sums_ref)
    push_blocks(work_ref, done, key_ref, weight_ref, from_ref, counts_ref, sums_ref)
    for spot in range(4):
        cut = slice(COLS * spot, COLS * spot + COLS)
        side_ref[cut, :] = sums_ref[spot].astype(BF16)
        own_ref[cut, :] = sums_ref[4 + spot]


def second_kernel(parts_ref, density_ref, side_ref, own_ref, stage_ref, key_ref, weight_ref, from_ref, counts_ref, sums_ref, work_ref, sem):
    pair, half, core, ahead = place()
    wide = 4 * COLS
    blocks = []
    for j in range(4):
        piece = parts_ref[j, wide : wide + 32, :].astype(F32)
        keys = piece[8:16] * float(BLOCK) + piece[0:8]
        for side in range(2):
            cut = slice(128 * side, 128 * side + 128)
            key_ref[2 * j + side] = keys[:, cut]
            weight_ref[2 * j + side] = piece[16:24, cut]
        whole = piece[24:32, :128].astype(jnp.int32)
        blocks += [j + whole[WIDTH * (j & 1) + s, 0] for s in range(WIDTH)]
    places, mine = split_work(blocks, half, ahead)
    done = list_work(work_ref, blocks, places, mine, 2)
    for j in range(4):
        cut = slice(COLS * j, COLS * j + COLS)
        one, two, three, four = (parts_ref[i, cut, :].astype(F32) for i in range(4))
        from_ref[j] = ((one + two) + (three + four)).astype(BF16)
    for part in range(2):
        stage_ref[:, BLOCK * part : BLOCK * part + BLOCK] = from_ref[2 * half + part]
    store = pltpu.make_async_copy(stage_ref, density_ref, sem)
    store.start()
    sums_ref[...] = jnp.zeros_like(sums_ref)
    push_blocks(work_ref, done, key_ref, weight_ref, from_ref, counts_ref, sums_ref)
    for spot in range(2):
        cut = slice(COLS * spot, COLS * spot + COLS)
        side_ref[cut, :] = sums_ref[spot].astype(BF16)
        own_ref[cut, :] = sums_ref[2 + spot]
    store.wait()


def last_kernel(both_ref, density_ref, stage_ref, sem):
    total = (both_ref[0].astype(F32) + both_ref[1].astype(F32)).astype(BF16)
    stage_ref[:, :BLOCK] = total[:COLS]
    stage_ref[:, BLOCK:] = total[COLS:]
    store = pltpu.make_async_copy(stage_ref, density_ref, sem)
    store.start()
    store.wait()


VMEM = pl.BlockSpec(memory_space=pltpu.VMEM)
ANY = pl.BlockSpec(memory_space=pl.ANY)


def call(kernel, name, outs, out_specs, scratch):
    return pl.pallas_call(
        kernel,
        out_shape=outs,
        out_specs=out_specs,
        scratch_shapes=scratch,
        compiler_params=pltpu.CompilerParams(vmem_limit_bytes=32 * 1024 * 1024),
        name=name,
    )


def shaped(*shape, dtype=F32):
    return jax.ShapeDtypeStruct(shape, dtype)


def body(density, offsets, *segments):
    boxes = lax.axis_size("box")
    rows = density.shape[0]
    count = segments[0].shape[-1]
    gather = functools.partial(lax.all_gather, axis_name=AXES)
    pair, half, core, ahead = place()

    lists, marks = call(
        sort_kernel,
        "sort",
        (shaped(32, 128), shaped(8, 128)),
        (VMEM, VMEM),
        [],
    )(*[member.reshape(count // 128, 128) for member in segments], offsets)
    lists = lax.all_gather(lists, "seg")
    side, own, meta = call(
        first_kernel,
        "first",
        (shaped(4 * COLS, BLOCK, dtype=BF16), shaped(4 * COLS, BLOCK), shaped(32, BLOCK, dtype=BF16)),
        (VMEM, VMEM, VMEM),
        [
            pltpu.VMEM((4, 8, 128), F32),
            pltpu.VMEM((4, 8, 128), F32),
            pltpu.VMEM((2, COLS, BLOCK), BF16),
            pltpu.VMEM((GROUP, BLOCK, BLOCK), BF16),
            pltpu.VMEM((9, COLS, BLOCK), F32),
            pltpu.SMEM((2 * WIDTH + GROUP,), jnp.int32),
        ],
    )(lists, density.T, marks)
    sides = gather(side, axis_index_groups=pair_groups(boxes))
    came = jnp.where(ahead == 1, sides[1], sides[0])
    mixed = (own + came.astype(F32)).astype(BF16)
    parts = gather(jnp.concatenate([mixed, meta], axis=0), axis_index_groups=half_groups(boxes))
    density_one, side, own = call(
        second_kernel,
        "second",
        (shaped(COLS, rows, dtype=BF16), shaped(2 * COLS, BLOCK, dtype=BF16), shaped(2 * COLS, BLOCK)),
        (ANY, VMEM, VMEM),
        [
            pltpu.VMEM((COLS, rows), BF16),
            pltpu.VMEM((8, 8, 128), F32),
            pltpu.VMEM((8, 8, 128), F32),
            pltpu.VMEM((4, COLS, BLOCK), BF16),
            pltpu.VMEM((GROUP, BLOCK, BLOCK), BF16),
            pltpu.VMEM((5, COLS, BLOCK), F32),
            pltpu.SMEM((4 * WIDTH + GROUP,), jnp.int32),
            pltpu.SemaphoreType.DMA,
        ],
    )(parts)
    sides = gather(side, axis_index_groups=pair_groups(boxes))
    came = jnp.where(ahead == 1, sides[1], sides[0])
    both = gather((own + came.astype(F32)).astype(BF16), axis_index_groups=core_groups(boxes))
    density_two = call(
        last_kernel,
        "last",
        shaped(COLS, rows, dtype=BF16),
        ANY,
        [pltpu.VMEM((COLS, rows), BF16), pltpu.SemaphoreType.DMA],
    )(both)
    return density_one.T, density_two.T


def solution(mesh):
    boxed = P("box", None)
    lined = P("box", "seg", None)
    return jax.shard_map(
        body,
        mesh=mesh,
        in_specs=(boxed, boxed) + (lined,) * 8,
        out_specs=(boxed, boxed),
        check_vma=False,
    )
```
